128 devices in a mesh: rows: 16 (over x, z), chan: 8 (over y, core).
Axes of the slice: x: 4, y: 4, z: 4, core: 2. Of those that a mesh axis runs over, the one named last changes fastest.
Arguments:
- frames: bfloat16 [2, 256, 128, 256], P(None, None, 'rows'), may hold values from -6 to 6
- hidden_init: bfloat16 [256, 128, 256], P('chan', 'rows'), may hold values from -3 to 3
- gate_weight: bfloat16 [3, 256, 9, 512], P(None, 'chan'), may hold values from -0.09375 to 0.09375
- readout: bfloat16 [256], P('chan'), may hold values from -1.5 to 1.5
- catchment: int32 [128, 256], P('rows'), may hold values from 0 to 511
- targets: float32 [512], replicated, may hold values from 0.2 to 2
Outputs:
- loss: float32 [], replicated
- gate_grad: float32 [3, 256, 9, 512], P(None, 'chan')
- readout_grad: float32 [256], P('chan')
- hidden_grad: float32 [256, 128, 256], P('chan', 'rows')
The draws below stay inside these ranges and needn't reach their ends.
All inputs are finite; a program needn't handle non-finite values.
Results may differ from the reference program's by a relative error of at most 0.007.
Values may be sent and summed in bfloat16 or wider, within the bound.
No kernel may reach another device: no remote copies, remote signals or barrier semaphores. Data moves between devices by JAX's collectives and lax.ppermute only.
A program may use at most 128 MiB of HBM per device.

```python
import math
import jax
import jax.numpy as jnp
import numpy as np
from jax import lax

C = 256
CIN = 256
STEPS = 2
COLS = 256
K = 512
H = 128


def touch_ends(drawn, own_key, low, largest):
    longest = drawn.shape.index(max(drawn.shape))
    spots = []
    for shift in (0, 1):
        where = [jax.random.randint(jax.random.fold_in(own_key, axis), (), 0, length) for axis, length in enumerate(drawn.shape)]
        where[longest] = (where[longest] + shift) % drawn.shape[longest]
        spots.append(tuple(where))
    return drawn.at[spots[0]].set(low).at[spots[1]].set(largest)


def shard_levels(key, extent, shards, smallest, high):
    factor_of, own = 1.0, jax.random.fold_in(key, 6)
    for axis_at, blocks in shards:
        steps = jnp.exp(jax.random.uniform(jax.random.fold_in(own, axis_at), (blocks,), jnp.float32, smallest / len(shards), high / len(shards)))
        factor_of = factor_of * jnp.repeat(steps, extent[axis_at] // blocks).reshape([-1 if axis == axis_at else 1 for axis in range(len(extent))])
    return factor_of


def cumulative_ranks(count, lean):
    loads = [(1 << 20) // math.isqrt(grade ** lean) + 1 for grade in range(1, count + 1)]
    scale = 1 + sum(loads) // (1 << 30)
    return np.cumsum(np.array([max(1, weight // scale) for weight in loads]))


def skewed_ids(rng, extent, number_of, slope):
    listing = cumulative_ranks(number_of, slope)
    ticket = jax.random.randint(jax.random.fold_in(rng, 1), extent, 0, int(listing[number_of - 1]))
    grade = jnp.searchsorted(jnp.asarray(listing, jnp.int32), ticket, side="right")
    return jax.random.permutation(jax.random.fold_in(rng, 2), number_of)[grade].astype(jnp.int32)


def centred(key, extent, scale, reach, split=(), kind=jnp.bfloat16):
    level = shard_levels(key, extent, split, -0.22, 0.18) if split else 1.0
    entries = jax.random.normal(key, extent, jnp.float32) * scale * level
    return jnp.minimum(jnp.maximum(entries, -reach), reach).astype(kind)


def setup_inputs(seed: int = 0) -> dict:
    seeds = jax.random.split(jax.random.key(seed), 7)
    return {
        "frames": centred(seeds[0], (STEPS, CIN, H, COLS), 1.0, 6.0, ((2, 16),)),
        "hidden_init": centred(seeds[1], (C, H, COLS), 0.5, 3.0, ((0, 8), (1, 16))),
        "gate_weight": centred(seeds[2], (3, C, 9, CIN + C), (9 * (CIN + C)) ** -0.5, 0.09375, ((1, 8),)),
        "readout": centred(seeds[3], (C,), 16 ** -0.5, 1.5, ((0, 8),)),
        "catchment": touch_ends(skewed_ids(seeds[4], (H, COLS), K, 2), jax.random.fold_in(seeds[4], 3), 0, K - 1).astype(jnp.int32),
        "targets": jnp.clip(jax.random.uniform(seeds[5], (K,), jnp.float32, 0.2, 2.0), 0.2, 2.0),
    }


def pad_field(field):
    widths = [(0, 0)] * (field.ndim - 2) + [(1, 1), (1, 1)]
    return jnp.pad(field, widths)


def conv_taps(kernel, padded):
    height = padded.shape[1] - 2
    width = padded.shape[2] - 2
    kernel_f = kernel.astype(jnp.float32)
    padded_f = padded.astype(jnp.float32)
    total = jnp.zeros((kernel.shape[0], kernel.shape[1], height, width), jnp.float32)
    for offset in range(9):
        shift_row, shift_col = offset // 3, offset % 3
        window = padded_f[:, shift_row:shift_row + height, shift_col:shift_col + width]
        total = total + jnp.einsum('goc,crw->gorw', kernel_f[:, :, offset], window)
    return total


def weight_taps(grad_pre, padded):
    height, width = grad_pre.shape[2], grad_pre.shape[3]
    grad_f = grad_pre.astype(jnp.float32)
    padded_f = padded.astype(jnp.float32)
    pieces = []
    for offset in range(9):
        shift_row, shift_col = offset // 3, offset % 3
        window = padded_f[:, shift_row:shift_row + height, shift_col:shift_col + width]
        pieces.append(jnp.einsum('gorw,crw->goc', grad_f, window))
    return jnp.stack(pieces, axis=2)


def input_taps(kernel, grad_pad):
    height = grad_pad.shape[2] - 2
    width = grad_pad.shape[3] - 2
    kernel_f = kernel.astype(jnp.float32)
    grad_f = grad_pad.astype(jnp.float32)
    total = jnp.zeros((kernel.shape[3], height, width), jnp.float32)
    for offset in range(9):
        shift_row, shift_col = offset // 3, offset % 3
        window = grad_f[:, :, 2 - shift_row:2 - shift_row + height, 2 - shift_col:2 - shift_col + width]
        total = total + jnp.einsum('goc,gorw->crw', kernel_f[:, :, offset], window)
    return total


def reference(frames, hidden_init, gate_weight, readout, catchment, targets):
    frame_depth = frames.shape[1]
    w_frame = gate_weight[..., :frame_depth]
    w_state = gate_weight[..., frame_depth:]
    state = hidden_init
    saved = []
    for step in range(STEPS):
        frame_pad = pad_field(frames[step])
        from_frame = conv_taps(w_frame, frame_pad)
        state_pad = pad_field(state)
        both = from_frame[0:2] + conv_taps(w_state[0:2], state_pad)
        update = jax.nn.sigmoid(both[0])
        reset = jax.nn.sigmoid(both[1])
        state_f = state.astype(jnp.float32)
        reset_state = (reset * state_f).astype(jnp.bfloat16)
        reset_pad = pad_field(reset_state)
        candidate = jnp.tanh(from_frame[2] + conv_taps(w_state[2:3], reset_pad)[0])
        saved.append((frame_pad, state_pad, reset_pad, state_f, update, reset, candidate))
        state = ((1.0 - update) * state_f + update * candidate).astype(jnp.bfloat16)
    state_f = state.astype(jnp.float32)
    rain = jnp.einsum('c,chw->hw', readout.astype(jnp.float32), state_f)
    labels = catchment.reshape(-1)
    onehot = (labels[:, None] == jnp.arange(K, dtype=jnp.int32)[None, :]).astype(jnp.float32)
    totals = jnp.dot(rain.reshape(-1), onehot, precision=lax.Precision.HIGHEST)
    counts = jnp.sum(onehot, axis=0)
    scale = 1.0 / (counts + 1.0)
    mean_rate = totals * scale
    rate = jax.nn.softplus(mean_rate)
    miss = rate - targets
    loss = 0.5 * jnp.mean(miss * miss)
    grad_mean = miss / K * jax.nn.sigmoid(mean_rate) * scale
    grad_rain = jnp.dot(onehot, grad_mean, precision=lax.Precision.HIGHEST).reshape(rain.shape)
    readout_grad = jnp.einsum('chw,hw->c', state_f, grad_rain)
    grad_state = readout.astype(jnp.float32)[:, None, None] * grad_rain[None]
    gate_grad = jnp.zeros(gate_weight.shape, jnp.float32)
    for step in reversed(range(STEPS)):
        frame_pad, state_pad, reset_pad, state_f, update, reset, candidate = saved[step]
        grad_update = grad_state * (candidate - state_f)
        grad_cand = grad_state * update
        carry = grad_state * (1.0 - update)
        pre_cand = (grad_cand * (1.0 - candidate * candidate)).astype(jnp.bfloat16)[None]
        cand_grad = jnp.concatenate([weight_taps(pre_cand, frame_pad), weight_taps(pre_cand, reset_pad)], axis=-1)
        grad_reset_state = input_taps(w_state[2:3], pad_field(pre_cand))
        grad_reset = grad_reset_state * state_f
        carry = carry + grad_reset_state * reset
        pre_both = jnp.stack([grad_update * update * (1.0 - update), grad_reset * reset * (1.0 - reset)]).astype(jnp.bfloat16)
        both_grad = jnp.concatenate([weight_taps(pre_both, frame_pad), weight_taps(pre_both, state_pad)], axis=-1)
        gate_grad = gate_grad + jnp.concatenate([both_grad, cand_grad], axis=0)
        grad_state = carry + input_taps(w_state[0:2], pad_field(pre_both))
    return loss, gate_grad, readout_grad, grad_state
```

```python
import functools

import jax
import jax.numpy as jnp
from jax import lax
from jax.experimental import pallas as pl
from jax.experimental.pallas import tpu as pltpu
from jax.sharding import PartitionSpec as P

BF = jnp.bfloat16
F32 = jnp.float32
PITCH = 48
RIM = 8
ROWS_IN = 24
PIX = ROWS_IN * PITCH
OWN_COLS = 32
OWN = 8 * OWN_COLS
C = 256
K = 512
SLOTS = 28
VMEM_LIMIT = 56 * 1024 * 1024


def sigmoid(x):
    return 0.5 * jnp.tanh(0.5 * x) + 0.5


def put(dst, row, count, lane, stride, left_first, x):
    before = pltpu.roll(x, 1, axis=0)
    after = pltpu.roll(x, count - 1, axis=0)
    order = (before, x, after) if left_first else (after, x, before)
    for b in range(3):
        dst[row : row + count, b * stride + lane : b * stride + lane + C] = order[b].astype(BF)


def own_pixels(x):
    return x.reshape(8, PITCH, C)[:, RIM : RIM + OWN_COLS].reshape(OWN, C)


def wide(lab):
    return jnp.concatenate([lab, lab], axis=1)


def conv(xc, w, gate, start, count):
    total = None
    for a in range(3):
        lhs = xc[pl.ds(start + (a - 1) * PITCH, count), :]
        rhs = jnp.concatenate([w[:, gate, 3 * a + b].reshape(C, 2 * C) for b in range(3)], axis=1)
        term = lax.dot_general(lhs, rhs, (((1,), (1,)), ((), ())), preferred_element_type=F32)
        total = term if total is None else total + term
    return total


def forward_kernel(
    x, w, lab, ro, u1, q1, c1, s1, u0, q0, c0, s2, v, tot, xc, ub, qb, sb
):
    def halo_block(field):
        return field.reshape(10, PITCH, C)[:, RIM : RIM + OWN_COLS].reshape(10 * OWN_COLS, C).astype(BF)

    sb[...] = x[2].astype(F32)
    for step in range(2):
        first = 1 + 2 * step
        count = (ROWS_IN - 2 * first) * PITCH
        start = first * PITCH
        put(xc, 0, PIX, 0, 2 * C, True, x[step].astype(F32))
        put(xc, 0, PIX, C, 2 * C, True, sb[...])
        piece = count // 3
        v[2 * step] = halo_block(sb[7 * PITCH : 17 * PITCH])
        for i in range(3):
            at = start + i * piece
            ub[at : at + piece] = sigmoid(conv(xc, w, 0, at, piece))
            qb[at : at + piece] = sigmoid(conv(xc, w, 1, at, piece))
        rs = (qb[start : start + count] * sb[start : start + count]).astype(BF).astype(F32)
        v[2 * step + 1] = halo_block(rs[(7 - first) * PITCH : (17 - first) * PITCH])
        put(xc, start, count, C, 2 * C, True, rs)
        start += PITCH
        count -= 2 * PITCH
        piece = count // 3
        for i in range(3):
            at = start + i * piece
            cand = jnp.tanh(conv(xc, w, 2, at, piece))
            u = ub[at : at + piece]
            s = sb[at : at + piece]
            nxt = (1.0 - u) * s + u * cand
            nxt = jnp.where(wide(lab[at : at + piece]) > 0, nxt, 0.0).astype(BF).astype(F32)
            if step == 0:
                lo, hi = max(at, 6 * PITCH), min(at + piece, 18 * PITCH)
                if lo < hi:
                    c0[lo - 6 * PITCH : hi - 6 * PITCH] = cand[lo - at : hi - at]
            else:
                c1[at - 4 * PITCH : at - 4 * PITCH + piece] = cand
                s1[at - 4 * PITCH : at - 4 * PITCH + piece] = s.astype(BF)
            qb_at = at
            sb[qb_at : qb_at + piece] = nxt
        if step == 0:
            u0[...] = ub[6 * PITCH : 18 * PITCH]
            q0[...] = qb[6 * PITCH : 18 * PITCH]
        else:
            u1[...] = ub[4 * PITCH : 20 * PITCH]
            q1[...] = qb[4 * PITCH : 20 * PITCH]
    last = sb[8 * PITCH : 16 * PITCH]
    s2[...] = last.astype(BF)
    rain = jnp.sum(last * ro[...], axis=1, keepdims=True)
    labels = lab[8 * PITCH : 16 * PITCH]
    column = lax.rem(lax.broadcasted_iota(jnp.int32, labels.shape, 0), PITCH)
    labels = jnp.where((column >= RIM) & (column < RIM + OWN_COLS), labels, 0)
    lanes = lax.broadcasted_iota(jnp.int32, labels.shape, 1) + 1
    for i in range(K // 128):
        hit = labels == lanes + 128 * i
        tot[i : i + 1] = jnp.sum(jnp.where(hit, rain, 0.0), axis=0, keepdims=True)
        tot[4 + i : 5 + i] = jnp.sum(jnp.where(hit, 1.0, 0.0), axis=0, keepdims=True)


def adjoint(px, w, gates, start, count):
    total = None
    width = len(gates) * C
    for a in range(3):
        lhs = px[pl.ds(start + (1 - a) * PITCH, count), : 3 * width]
        rhs = jnp.concatenate(
            [w[:, g, 3 * a + b, :, C:].reshape(C, C) for b in range(3) for g in gates], axis=0
        )
        term = jnp.dot(lhs, rhs, preferred_element_type=F32)
        total = term if total is None else total + term
    return total


def backward_kernel(
    tp, tgt, w, lab, ro, u1, q1, c1, s1, u0, q0, c0, s0, s2, msg, loss, px, gs
):
    sums = jnp.sum(tp[...], axis=0)
    scale = 1.0 / (sums[4:8] + 1.0)
    mean = sums[0:4] * scale
    rate = jnp.maximum(mean, 0.0) + jnp.log1p(jnp.exp(-jnp.abs(mean)))
    miss = rate - tgt[...]
    loss[...] = jnp.broadcast_to(0.5 / K * jnp.sum(miss * miss), (8, 128))
    gm = miss * (1.0 / K) * (1.0 / (1.0 + jnp.exp(-mean))) * scale

    labels = lab[4 * PITCH : 20 * PITCH]
    lanes = lax.broadcasted_iota(jnp.int32, labels.shape, 1) + 1
    grain = jnp.zeros(labels.shape, F32)
    for i in range(K // 128):
        grain += jnp.where(labels == lanes + 128 * i, gm[i : i + 1], 0.0)
    grain = jnp.sum(grain, axis=1, keepdims=True)
    gs[4 * PITCH : 20 * PITCH] = grain * ro[...]
    part = s2[...].astype(F32) * grain[4 * PITCH : 12 * PITCH]
    column = lax.rem(lax.broadcasted_iota(jnp.int32, part.shape, 0), PITCH)
    part = jnp.where((column >= RIM) & (column < RIM + OWN_COLS), part, 0.0)
    part = jnp.sum(part, axis=0, keepdims=True)
    part_hi = part.astype(BF).astype(F32)
    tail = lax.broadcasted_iota(jnp.int32, (16, C), 0)
    tail = jnp.where(tail == 0, part_hi, jnp.where(tail == 1, part - part_hi, 0.0)).astype(BF)
    for j in range(8):
        msg[j, 224:240] = tail

    def send(slot, field):
        turned = own_pixels(field).T.astype(BF)
        for j in range(8):
            msg[j, slot * 32 : slot * 32 + 32] = turned[j * 32 : j * 32 + 32]

    for step in (1, 0):
        first = 4 if step == 1 else 6
        rows = ROWS_IN - 2 * first
        uv, qv, cv = (u1, q1, c1) if step == 1 else (u0, q0, c0)

        def state(lo, hi):
            if step == 1:
                return s1[(lo - 4) * PITCH : (hi - 4) * PITCH].astype(F32)
            return s0[lo * PITCH : hi * PITCH].astype(F32)

        def at(ref, lo, hi):
            return ref[(lo - first) * PITCH : (hi - first) * PITCH]

        lo, hi = first, first + rows
        g = gs[lo * PITCH : hi * PITCH]
        cand = cv[...]
        pc = (g * uv[...] * (1.0 - cand * cand)).astype(BF).astype(F32)
        put(px, lo * PITCH, rows * PITCH, 0, C, False, pc)
        send(step * 3 + 2, pc[(8 - lo) * PITCH : (16 - lo) * PITCH])
        lo, hi = lo + 1, hi - 1
        n = (hi - lo) * PITCH
        grs = adjoint(px, w, (2,), lo * PITCH, n)
        s = state(lo, hi)
        g = gs[lo * PITCH : hi * PITCH]
        u, q, cand = at(uv, lo, hi), at(qv, lo, hi), at(cv, lo, hi)
        pu = (g * (cand - s) * u * (1.0 - u)).astype(BF).astype(F32)
        pq = (grs * s * q * (1.0 - q)).astype(BF).astype(F32)
        gs[lo * PITCH : hi * PITCH] = g * (1.0 - u) + grs * q
        put(px, lo * PITCH, n, 0, 2 * C, False, pu)
        put(px, lo * PITCH, n, C, 2 * C, False, pq)
        send(step * 3, pu[(8 - lo) * PITCH : (16 - lo) * PITCH])
        send(step * 3 + 1, pq[(8 - lo) * PITCH : (16 - lo) * PITCH])
        lo, hi = lo + 1, hi - 1
        n = (hi - lo) * PITCH
        g = gs[lo * PITCH : hi * PITCH] + adjoint(px, w, (0, 1), lo * PITCH, n)
        g = jnp.where(wide(lab[lo * PITCH : hi * PITCH]) > 0, g, 0.0)
        if step == 1:
            gs[lo * PITCH : hi * PITCH] = g
        else:
            send(6, g)


def corr_kernel(r, vf, vs, out, p3):
    def lanes_of(j, t):
        return r[j, t * 96 : t * 96 + 96, :].astype(F32)

    column = lax.rem(lax.broadcasted_iota(jnp.int32, (96, OWN), 1), OWN_COLS)
    for t in range(2):
        for j in range(8):
            here = lanes_of(j, t)
            nxt = pltpu.roll(here, OWN - 1, axis=1)
            prv = pltpu.roll(here, 1, axis=1)
            over = pltpu.roll(lanes_of(j + 1, t), OWN_COLS - 1, axis=1) if j < 7 else jnp.zeros_like(here)
            under = pltpu.roll(lanes_of(j - 1, t), OWN - OWN_COLS + 1, axis=1) if j > 0 else jnp.zeros_like(here)
            nxt = jnp.where(column == OWN_COLS - 1, over, nxt)
            prv = jnp.where(column == 0, under, prv)
            at = (t * 8 + j) * OWN
            for b, field in enumerate((nxt, here, prv)):
                for g in range(3):
                    p3[g * 96 + b * 32 : g * 96 + b * 32 + 32, at : at + OWN] = field[
                        g * 32 : g * 32 + 32
                    ].astype(BF)

    def store(g, a, value, half):
        for b in range(3):
            slot = g * 9 + 3 * a + b
            for l in range(2):
                lane = half * 2 + l
                out[lane * 4 + slot // 7, (slot % 7) * 32 : (slot % 7) * 32 + 32] = value[
                    b * 32 : b * 32 + 32, l * 128 : l * 128 + 128
                ].astype(BF)

    order = [(t, j) for t in range(2) for j in range(8)]
    for a in range(3):
        field = jnp.concatenate(
            [vf[t, a : a + 8, j].reshape(OWN, C) for t, j in order], axis=0
        )
        value = jnp.dot(p3[...], field, preferred_element_type=F32)
        for g in range(3):
            store(g, a, value[g * 96 : g * 96 + 96], 0)
        field = jnp.concatenate([vs[j, 2 * t, a * 32 : a * 32 + OWN] for t, j in order], axis=0)
        value = jnp.dot(p3[0:192], field, preferred_element_type=F32)
        for g in range(2):
            store(g, a, value[g * 96 : g * 96 + 96], 1)
        field = jnp.concatenate([vs[j, 2 * t + 1, a * 32 : a * 32 + OWN] for t, j in order], axis=0)
        value = jnp.dot(p3[192:288], field, preferred_element_type=F32)
        store(2, a, value, 1)

    tail = jnp.sum(r[:, 224:240, :].astype(F32), axis=0)
    part = tail[0:1] + tail[1:2]
    part_hi = part.astype(BF).astype(F32)
    row = lax.broadcasted_iota(jnp.int32, (32, C), 0)
    last = jnp.where(row == 0, part_hi, jnp.where(row == 1, part - part_hi, 0.0)).astype(BF)
    for l in range(2):
        out[l * 4 + 3, 192:224] = last[:, l * 128 : l * 128 + 128]
        out[l * 4 + 11, 192:224] = jnp.zeros((32, 128), BF)


def call(kernel, outs, scratch, flops, moved, *args):
    return pl.pallas_call(
        kernel,
        out_shape=outs,
        in_specs=[pl.BlockSpec(memory_space=pltpu.VMEM)] * len(args),
        out_specs=jax.tree.map(lambda _: pl.BlockSpec(memory_space=pltpu.VMEM), outs),
        scratch_shapes=scratch,
        compiler_params=pltpu.CompilerParams(vmem_limit_bytes=VMEM_LIMIT),
        cost_estimate=pl.CostEstimate(flops=flops, bytes_accessed=moved, transcendentals=0),
    )(*args)


def shape(*dims, dtype=F32):
    return jax.ShapeDtypeStruct(dims, dtype)


def columns_window(field, axis, at):
    widths = [(0, 0)] * field.ndim
    widths[axis] = (RIM, RIM)
    return lax.dynamic_slice_in_dim(jnp.pad(field, widths), at, PITCH, axis=axis)


def per_device(frames, hidden_init, gate_weight, readout, catchment, targets):
    chan = lax.axis_index("chan")
    row_tile = lax.axis_index("rows")
    up = [(i, i + 1) for i in range(15)]
    down = [(i + 1, i) for i in range(15)]

    weights = lax.all_gather(jnp.transpose(gate_weight, (0, 2, 1, 3)), "chan", axis=0)

    padded = jnp.pad(hidden_init, ((0, 0), (0, 0), (RIM, RIM)))
    pieces = jnp.stack([padded[:, :, 32 * j : 32 * j + PITCH] for j in range(8)])
    own_readout = jnp.broadcast_to(jnp.pad(readout, (0, 8 * PITCH - 32)), (8, 1, 8 * PITCH))
    pieces = jnp.concatenate([pieces.reshape(8, 32, 8 * PITCH), own_readout], axis=1)
    pieces = lax.all_to_all(pieces, "chan", 0, 0)
    ro = pieces[:, 32, :32].reshape(1, C).astype(F32)
    state = jnp.transpose(pieces[:, :32].reshape(C, 8, PITCH), (1, 2, 0))
    turned = jnp.transpose(frames, (0, 2, 3, 1))
    middle = jnp.concatenate([columns_window(turned, 2, 32 * chan), state[None]], axis=0)
    above = lax.ppermute(middle, "rows", up)
    below = lax.ppermute(middle, "rows", down)
    x = jnp.concatenate([above, middle, below], axis=1).reshape(3, PIX, C)
    frame_above = lax.ppermute(turned[:, 7:8], "rows", up)
    frame_below = lax.ppermute(turned[:, 0:1], "rows", down)
    vf = jnp.concatenate([frame_above, turned, frame_below], axis=1).reshape(2, 10, 8, OWN_COLS, C)
    labels = catchment + 1
    labels = jnp.concatenate(
        [lax.ppermute(labels, "rows", up), labels, lax.ppermute(labels, "rows", down)], axis=0
    )
    labels = columns_window(labels, 1, 32 * chan).reshape(PIX, 1)
    labels = jnp.broadcast_to(labels, (PIX, 128))

    n1, n0 = 16 * PITCH, 12 * PITCH
    u1, q1, c1, s1, u0, q0, c0, s2, v, tot = call(
        forward_kernel,
        (
            shape(n1, C), shape(n1, C), shape(n1, C), shape(n1, C, dtype=BF),
            shape(n0, C), shape(n0, C), shape(n0, C), shape(8 * PITCH, C, dtype=BF),
            shape(4, 10 * OWN_COLS, C, dtype=BF), shape(8, 128),
        ),
        [pltpu.VMEM((PIX, 6 * C), BF)] + [pltpu.VMEM((PIX, C), F32)] * 3,
        13_000_000_000, 20_000_000,
        x, weights, labels, ro,
    )
    vs = lax.all_gather(v, "chan", axis=0)
    tp = lax.all_to_all(jnp.broadcast_to(tot[None], (128, 8, 128)), ("rows", "chan"), 0, 0)
    msg, loss = call(
        backward_kernel,
        (shape(8, 240, C, dtype=BF), shape(8, 128)),
        [pltpu.VMEM((PIX, 6 * C), BF), pltpu.VMEM((PIX, C), F32)],
        4_000_000_000, 20_000_000,
        tp, targets.reshape(4, 128), weights, labels, ro, u1, q1, c1, s1, u0, q0, c0, x[2], s2,
    )
    got = lax.all_to_all(msg, "chan", 0, 0)
    hidden_grad = got[:, 192:224].reshape(8, 32, 8, OWN_COLS)
    hidden_grad = jnp.transpose(hidden_grad, (1, 2, 0, 3)).reshape(32, 8, 8 * OWN_COLS).astype(F32)
    part = call(
        corr_kernel,
        shape(16, 224, 128, dtype=BF),
        [pltpu.VMEM((288, 16 * OWN), BF)],
        4_000_000_000, 10_000_000,
        got, vf, vs,
    )
    mine = lax.all_to_all(part, "rows", 0, 0)
    mine = jnp.sum(mine.astype(F32), axis=0)
    tail = mine[192:193] + mine[193:194]
    tail_hi = tail.astype(BF).astype(F32)
    tail = jnp.concatenate([mine[:192], tail_hi, tail - tail_hi, mine[194:]], axis=0)
    mine = jnp.where(row_tile % 4 == 3, tail, mine).astype(BF)
    whole = lax.all_to_all(jnp.broadcast_to(mine[None], (16, 224, 128)), "rows", 0, 0)
    whole = whole.astype(F32).reshape(4, 4, 7, 32, 128)
    whole = jnp.transpose(whole, (1, 2, 3, 0, 4)).reshape(SLOTS, 32, 2 * C)
    gate_grad = jnp.transpose(whole[:27].reshape(3, 9, 32, 2 * C), (0, 2, 1, 3))
    readout_grad = whole[27, 0, :C] + whole[27, 1, :C]
    readout_grad = lax.dynamic_slice_in_dim(readout_grad, chan * 32, 32)
    return (loss[0, 0], gate_grad, readout_grad, hidden_grad)


def solution(mesh):
    in_specs = (
        P(None, None, "rows", None),
        P("chan", "rows", None),
        P(None, "chan", None, None),
        P("chan"),
        P("rows", None),
        P(),
    )
    out_specs = (P(), P(None, "chan", None, None), P("chan"), P("chan", "rows", None))
    return jax.shard_map(
        per_device, mesh=mesh, in_specs=in_specs, out_specs=out_specs, check_vma=False
    )
```

```python
import functools

import jax
import jax.numpy as jnp
from jax import lax
from jax.experimental import pallas as pl
from jax.experimental.pallas import tpu as pltpu
from jax.sharding import PartitionSpec as P

BF = jnp.bfloat16
F32 = jnp.float32
PITCH = 48
RIM = 8
ROWS_IN = 24
PIX = ROWS_IN * PITCH
OWN_COLS = 32
OWN = 8 * OWN_COLS
C = 256
K = 512
CUTS = 2
V_ROWS = 10 * OWN_COLS
V_ALL = 4 * V_ROWS + 4 * OWN_COLS
VMEM_LIMIT = 56 * 1024 * 1024


def sigmoid(x):
    return 0.5 * jnp.tanh(0.5 * x) + 0.5


class Taps:
    def __init__(self, ref):
        self.ref = ref

    def rows(self, gate, tap):
        block = self.ref[:, gate * 9 + tap]
        return block.reshape(C, block.shape[-1])


def put(dst, row, count, lane, stride, left_first, x):
    before = pltpu.roll(x, 1, axis=0)
    after = pltpu.roll(x, count - 1, axis=0)
    order = (before, x, after) if left_first else (after, x, before)
    for b in range(3):
        dst[row : row + count, b * stride + lane : b * stride + lane + C] = order[b].astype(BF)


def own_pixels(x):
    return x.reshape(8, PITCH, C)[:, RIM : RIM + OWN_COLS].reshape(OWN, C)


def wide(lab):
    return jnp.concatenate([lab, lab], axis=1)


def conv(xc, w, gates, start, count):
    total = None
    for a in range(3):
        lhs = xc[pl.ds(start + (a - 1) * PITCH, count), :]
        rhs = [jnp.concatenate([w.rows(g, 3 * a + b) for b in range(3)], axis=1) for g in gates]
        rhs = jnp.concatenate(rhs, axis=0) if len(rhs) > 1 else rhs[0]
        term = lax.dot_general(lhs, rhs, (((1,), (1,)), ((), ())), preferred_element_type=F32)
        total = term if total is None else total + term
    return total


def forward_kernel(
    above, middle, below, lab, ro, kernels,
    u1, q1, c1, s1, u0, q0, c0, s0, s2, v, tot, w4, xc, ub, qb, sb, sem
):
    copy = pltpu.make_async_copy(kernels, w4, sem)
    copy.start()
    w = Taps(w4)

    def window(k):
        parts = [ref[k * 8 * PITCH : (k + 1) * 8 * PITCH].astype(F32) for ref in (above, middle, below)]
        return jnp.concatenate(parts, axis=0)

    def halo_block(field):
        return field.reshape(10, PITCH, C)[:, RIM : RIM + OWN_COLS].reshape(10 * OWN_COLS, C).astype(BF)

    for step in range(2):
        for n, ref in enumerate((above, below)):
            line = (step * 8 + 7 - 7 * n) * PITCH
            at = 4 * V_ROWS + (2 * step + n) * OWN_COLS
            v[at : at + OWN_COLS] = ref[line : line + PITCH].astype(F32)[RIM : RIM + OWN_COLS].astype(BF)
    sb[...] = window(2)
    for step in range(2):
        first = 1 + 2 * step
        count = (ROWS_IN - 2 * first) * PITCH
        start = first * PITCH
        put(xc, 0, PIX, 0, 2 * C, True, window(step))
        put(xc, 0, PIX, C, 2 * C, True, sb[...])
        piece = count // CUTS
        v[2 * step * V_ROWS : (2 * step + 1) * V_ROWS] = halo_block(sb[7 * PITCH : 17 * PITCH])
        if step == 0:
            copy.wait()
        for i in range(CUTS):
            at = start + i * piece
            both = sigmoid(conv(xc, w, (0, 1), at, piece))
            ub[at : at + piece] = both[:, :C]
            qb[at : at + piece] = both[:, C:]
        rs = (qb[start : start + count] * sb[start : start + count]).astype(BF).astype(F32)
        v[(2 * step + 1) * V_ROWS : (2 * step + 2) * V_ROWS] = halo_block(rs[(7 - first) * PITCH : (17 - first) * PITCH])
        put(xc, start, count, C, 2 * C, True, rs)
        start += PITCH
        count -= 2 * PITCH
        piece = count // CUTS
        for i in range(CUTS):
            at = start + i * piece
            cand = jnp.tanh(conv(xc, w, (2,), at, piece))
            u = ub[at : at + piece]
            s = sb[at : at + piece]
            nxt = (1.0 - u) * s + u * cand
            nxt = jnp.where(wide(lab[at : at + piece]) > 0, nxt, 0.0).astype(BF).astype(F32)
            if step == 0:
                lo, hi = max(at, 6 * PITCH), min(at + piece, 18 * PITCH)
                if lo < hi:
                    c0[lo - 6 * PITCH : hi - 6 * PITCH] = cand[lo - at : hi - at]
            else:
                c1[at - 4 * PITCH : at - 4 * PITCH + piece] = cand
                s1[at - 4 * PITCH : at - 4 * PITCH + piece] = s.astype(BF)
            qb_at = at
            sb[qb_at : qb_at + piece] = nxt
        if step == 0:
            s0[...] = window(2)[6 * PITCH : 18 * PITCH].astype(BF)
            u0[...] = ub[6 * PITCH : 18 * PITCH]
            q0[...] = qb[6 * PITCH : 18 * PITCH]
        else:
            u1[...] = ub[4 * PITCH : 20 * PITCH]
            q1[...] = qb[4 * PITCH : 20 * PITCH]
    last = sb[8 * PITCH : 16 * PITCH]
    s2[...] = last.astype(BF)
    rain = jnp.sum(last * ro[...], axis=1, keepdims=True)
    labels = lab[8 * PITCH : 16 * PITCH]
    column = lax.rem(lax.broadcasted_iota(jnp.int32, labels.shape, 0), PITCH)
    labels = jnp.where((column >= RIM) & (column < RIM + OWN_COLS), labels, 0)
    lanes = lax.broadcasted_iota(jnp.int32, labels.shape, 1) + 1
    totals, counts = [], []
    for i in range(K // 128):
        hit = labels == lanes + 128 * i
        totals.append(jnp.sum(jnp.where(hit, rain, 0.0), axis=0, keepdims=True))
        counts.append(jnp.sum(jnp.where(hit, 1.0, 0.0), axis=0, keepdims=True))
    tot[...] = jnp.broadcast_to(jnp.concatenate(totals + counts, axis=0)[None], tot.shape)


def adjoint(px, w, gates, start, count):
    total = None
    width = len(gates) * C
    for a in range(3):
        lhs = px[pl.ds(start + (1 - a) * PITCH, count), : 3 * width]
        rhs = jnp.concatenate(
            [w.rows(g, 3 * a + b) for b in range(3) for g in gates], axis=0
        )
        term = jnp.dot(lhs, rhs, preferred_element_type=F32)
        total = term if total is None else total + term
    return total


def backward_kernel(
    tp, tgt, lab, ro, u1, q1, c1, s1, u0, q0, c0, s0, s2, kernels, msg, loss, w4, px, gs, sem
):
    copy = pltpu.make_async_copy(kernels.at[:, :, :, C:], w4, sem)
    copy.start()
    w = Taps(w4)
    sums = jnp.sum(tp[...], axis=0)
    scale = 1.0 / (sums[4:8] + 1.0)
    mean = sums[0:4] * scale
    rate = jnp.maximum(mean, 0.0) + jnp.log1p(jnp.exp(-jnp.abs(mean)))
    miss = rate - tgt[...]
    loss[...] = jnp.broadcast_to(0.5 / K * jnp.sum(miss * miss), (8, 128))
    gm = miss * (1.0 / K) * (1.0 / (1.0 + jnp.exp(-mean))) * scale

    labels = lab[4 * PITCH : 20 * PITCH]
    lanes = lax.broadcasted_iota(jnp.int32, labels.shape, 1) + 1
    grain = jnp.zeros(labels.shape, F32)
    for i in range(K // 128):
        grain += jnp.where(labels == lanes + 128 * i, gm[i : i + 1], 0.0)
    grain = jnp.sum(grain, axis=1, keepdims=True)
    gs[4 * PITCH : 20 * PITCH] = grain * ro[...]
    part = s2[...].astype(F32) * grain[4 * PITCH : 12 * PITCH]
    column = lax.rem(lax.broadcasted_iota(jnp.int32, part.shape, 0), PITCH)
    part = jnp.where((column >= RIM) & (column < RIM + OWN_COLS), part, 0.0)
    part = jnp.sum(part, axis=0, keepdims=True)
    part_hi = part.astype(BF).astype(F32)
    tail = lax.broadcasted_iota(jnp.int32, (16, C), 0)
    tail = jnp.where(tail == 0, part_hi, jnp.where(tail == 1, part - part_hi, 0.0)).astype(BF)
    for j in range(8):
        msg[j, 224:240] = tail

    def send(slot, field):
        turned = own_pixels(field).T.astype(BF)
        for j in range(8):
            msg[j, slot * 32 : slot * 32 + 32] = turned[j * 32 : j * 32 + 32]

    for step in (1, 0):
        first = 4 if step == 1 else 6
        rows = ROWS_IN - 2 * first
        uv, qv, cv = (u1, q1, c1) if step == 1 else (u0, q0, c0)

        def state(lo, hi):
            if step == 1:
                return s1[(lo - 4) * PITCH : (hi - 4) * PITCH].astype(F32)
            return s0[(lo - 6) * PITCH : (hi - 6) * PITCH].astype(F32)

        def at(ref, lo, hi):
            return ref[(lo - first) * PITCH : (hi - first) * PITCH]

        lo, hi = first, first + rows
        g = gs[lo * PITCH : hi * PITCH]
        cand = cv[...]
        pc = (g * uv[...] * (1.0 - cand * cand)).astype(BF).astype(F32)
        put(px, lo * PITCH, rows * PITCH, 0, C, False, pc)
        send(step * 3 + 2, pc[(8 - lo) * PITCH : (16 - lo) * PITCH])
        lo, hi = lo + 1, hi - 1
        n = (hi - lo) * PITCH
        if step == 1:
            copy.wait()
        grs = adjoint(px, w, (2,), lo * PITCH, n)
        s = state(lo, hi)
        g = gs[lo * PITCH : hi * PITCH]
        u, q, cand = at(uv, lo, hi), at(qv, lo, hi), at(cv, lo, hi)
        pu = (g * (cand - s) * u * (1.0 - u)).astype(BF).astype(F32)
        pq = (grs * s * q * (1.0 - q)).astype(BF).astype(F32)
        gs[lo * PITCH : hi * PITCH] = g * (1.0 - u) + grs * q
        put(px, lo * PITCH, n, 0, 2 * C, False, pu)
        put(px, lo * PITCH, n, C, 2 * C, False, pq)
        send(step * 3, pu[(8 - lo) * PITCH : (16 - lo) * PITCH])
        send(step * 3 + 1, pq[(8 - lo) * PITCH : (16 - lo) * PITCH])
        lo, hi = lo + 1, hi - 1
        n = (hi - lo) * PITCH
        g = gs[lo * PITCH : hi * PITCH] + adjoint(px, w, (0, 1), lo * PITCH, n)
        g = jnp.where(wide(lab[lo * PITCH : hi * PITCH]) > 0, g, 0.0)
        if step == 1:
            gs[lo * PITCH : hi * PITCH] = g
        else:
            send(6, g)


def corr_kernel(r, frames, gathered, out, vs, vf, p3, sems):
    copies = [
        pltpu.make_async_copy(frames, vf, sems.at[0]),
        pltpu.make_async_copy(gathered, vs, sems.at[1]),
    ]
    for copy in copies:
        copy.start()

    def lanes_of(j, t):
        return r[j, t * 96 : t * 96 + 96, :].astype(F32)

    column = lax.rem(lax.broadcasted_iota(jnp.int32, (96, OWN), 1), OWN_COLS)
    for t in range(2):
        for j in range(8):
            here = lanes_of(j, t)
            nxt = pltpu.roll(here, OWN - 1, axis=1)
            prv = pltpu.roll(here, 1, axis=1)
            over = pltpu.roll(lanes_of(j + 1, t), OWN_COLS - 1, axis=1) if j < 7 else jnp.zeros_like(here)
            under = pltpu.roll(lanes_of(j - 1, t), OWN - OWN_COLS + 1, axis=1) if j > 0 else jnp.zeros_like(here)
            nxt = jnp.where(column == OWN_COLS - 1, over, nxt)
            prv = jnp.where(column == 0, under, prv)
            at = (t * 8 + j) * OWN
            for b, field in enumerate((nxt, here, prv)):
                for g in range(3):
                    p3[g * 96 + b * 32 : g * 96 + b * 32 + 32, at : at + OWN] = field[
                        g * 32 : g * 32 + 32
                    ].astype(BF)

    for copy in copies:
        copy.wait()

    def store(g, a, value, half):
        for b in range(3):
            slot = g * 9 + 3 * a + b
            for l in range(2):
                lane = half * 2 + l
                out[lane * 4 + slot // 7, (slot % 7) * 32 : (slot % 7) * 32 + 32] = value[
                    b * 32 : b * 32 + 32, l * 128 : l * 128 + 128
                ].astype(BF)

    def frame_rows(t, j, a):
        at = 4 * V_ROWS + 2 * t * OWN_COLS
        if a == 0:
            return vs[j, at : at + OWN_COLS], vf[t, 0:7, j].reshape(7 * OWN_COLS, C)
        if a == 1:
            return (vf[t, :, j].reshape(OWN, C),)
        return vf[t, 1:8, j].reshape(7 * OWN_COLS, C), vs[j, at + OWN_COLS : at + 2 * OWN_COLS]

    order = [(t, j) for t in range(2) for j in range(8)]
    for a in range(3):
        field = jnp.concatenate([part for t, j in order for part in frame_rows(t, j, a)], axis=0)
        value = jnp.dot(p3[...], field, preferred_element_type=F32)
        for g in range(3):
            store(g, a, value[g * 96 : g * 96 + 96], 0)
        field = jnp.concatenate([vs[j, pl.ds(2 * t * V_ROWS + a * OWN_COLS, OWN)] for t, j in order], axis=0)
        value = jnp.dot(p3[0:192], field, preferred_element_type=F32)
        for g in range(2):
            store(g, a, value[g * 96 : g * 96 + 96], 1)
        field = jnp.concatenate([vs[j, pl.ds((2 * t + 1) * V_ROWS + a * OWN_COLS, OWN)] for t, j in order], axis=0)
        value = jnp.dot(p3[192:288], field, preferred_element_type=F32)
        store(2, a, value, 1)

    tail = jnp.sum(r[:, 224:240, :].astype(F32), axis=0)
    part = tail[0:1] + tail[1:2]
    part_hi = part.astype(BF).astype(F32)
    row = lax.broadcasted_iota(jnp.int32, (32, C), 0)
    last = jnp.where(row == 0, part_hi, jnp.where(row == 1, part - part_hi, 0.0)).astype(BF)
    for l in range(2):
        out[l * 4 + 3, 192:224] = last[:, l * 128 : l * 128 + 128]
        out[l * 4 + 11, 192:224] = jnp.zeros((32, 128), BF)


def finish_sum_kernel(last, parts, out):
    total = parts[0].astype(F32)
    for n in range(1, 16):
        total = total + parts[n].astype(F32)
    pair = total[192:193] + total[193:194]
    pair_hi = pair.astype(BF).astype(F32)
    row = lax.broadcasted_iota(jnp.int32, total.shape, 0)
    split = jnp.where(row == 192, pair_hi, jnp.where(row == 193, pair - pair_hi, total))
    total = jnp.where(last[0] == 1, split, total).astype(BF)
    out[...] = jnp.broadcast_to(total[None], out.shape)


def layout_kernel(parts, grad, readout):
    for lane in range(4):
        for group in range(4):
            block = parts[lane * 4 + group].astype(F32).reshape(7, 32, 128)
            count = min(7, 27 - group * 7)
            grad[group * 7 : group * 7 + count, :, lane * 128 : lane * 128 + 128] = block[:count]
            if group == 3 and lane < 2:
                readout[:, lane * 128 : lane * 128 + 128] = block[6, 0:1] + block[6, 1:2]


VM = pl.BlockSpec(memory_space=pltpu.VMEM)
SM = pl.BlockSpec(memory_space=pltpu.SMEM)
HB = pl.BlockSpec(memory_space=pl.ANY)


def call(kernel, specs, outs, scratch, flops, moved, *args, limit=VMEM_LIMIT):
    return pl.pallas_call(
        kernel,
        out_shape=outs,
        in_specs=specs,
        out_specs=jax.tree.map(lambda _: VM, outs),
        scratch_shapes=scratch,
        compiler_params=pltpu.CompilerParams(vmem_limit_bytes=limit),
        cost_estimate=pl.CostEstimate(flops=flops, bytes_accessed=moved, transcendentals=0),
    )(*args)


def shape(*dims, dtype=F32):
    return jax.ShapeDtypeStruct(dims, dtype)


def columns_window(field, axis, at):
    widths = [(0, 0)] * field.ndim
    widths[axis] = (RIM, RIM)
    return lax.dynamic_slice_in_dim(jnp.pad(field, widths), at, PITCH, axis=axis)


def per_device(frames, hidden_init, gate_weight, readout, catchment, targets):
    chan = lax.axis_index("chan")
    row_tile = lax.axis_index("rows")
    up = [(i, i + 1) for i in range(15)]
    down = [(i + 1, i) for i in range(15)]

    padded = jnp.pad(hidden_init, ((0, 0), (0, 0), (RIM, RIM)))
    pieces = jnp.stack([padded[:, :, 32 * j : 32 * j + PITCH] for j in range(8)])
    own_readout = jnp.broadcast_to(jnp.pad(readout, (0, 8 * PITCH - 32)), (8, 1, 8 * PITCH))
    pieces = jnp.concatenate([pieces.reshape(8, 32, 8 * PITCH), own_readout], axis=1)
    own_kernel = jnp.transpose(gate_weight, (0, 2, 1, 3)).reshape(27, 32, 2 * C)
    kernels = lax.all_gather(own_kernel, "chan", axis=0)
    pieces = lax.all_to_all(pieces, "chan", 0, 0)
    turned = jnp.transpose(frames, (0, 2, 3, 1))
    ro = pieces[:, 32, :32].reshape(1, C).astype(F32)
    state = jnp.transpose(pieces[:, :32].reshape(C, 8 * PITCH))
    labels = columns_window(catchment + 1, 1, 32 * chan).reshape(-1)
    digits = jnp.concatenate([labels // 256, labels % 256]).astype(BF).reshape(3, C)
    middle = columns_window(turned, 2, 32 * chan).reshape(16 * PITCH, C)
    middle = jnp.concatenate([middle, state, jnp.pad(digits, ((0, 13), (0, 0)))], axis=0)
    above = lax.ppermute(middle, "rows", up)
    below = lax.ppermute(middle, "rows", down)
    digits = jnp.stack([part[24 * PITCH : 24 * PITCH + 3] for part in (above, middle, below)])
    digits = digits.reshape(3, 2, 8 * PITCH).astype(jnp.int32)
    labels = (digits[:, 0] * 256 + digits[:, 1]).reshape(PIX, 1)
    labels = jnp.broadcast_to(labels, (PIX, 128))

    n1, n0 = 16 * PITCH, 12 * PITCH
    dma = pltpu.SemaphoreType.DMA(())
    u1, q1, c1, s1, u0, q0, c0, s0, s2, v, tot = call(
        forward_kernel,
        [VM] * 5 + [HB],
        (
            shape(n1, C), shape(n1, C), shape(n1, C), shape(n1, C, dtype=BF),
            shape(n0, C), shape(n0, C), shape(n0, C), shape(n0, C, dtype=BF), shape(8 * PITCH, C, dtype=BF),
            shape(V_ALL, C, dtype=BF), shape(128, 8, 128),
        ),
        [pltpu.VMEM((8, 27, 32, 2 * C), BF), pltpu.VMEM((PIX, 6 * C), BF)] + [pltpu.VMEM((PIX, C), F32)] * 3 + [dma],
        13_000_000_000, 20_000_000,
        above, middle, below, labels, ro, kernels,
    )
    tp = lax.all_to_all(tot, ("rows", "chan"), 0, 0)
    vs = lax.all_gather(v, "chan", axis=0)
    msg, loss = call(
        backward_kernel,
        [VM] * 13 + [HB],
        (shape(8, 240, C, dtype=BF), shape(8, 128)),
        [pltpu.VMEM((8, 27, 32, C), BF), pltpu.VMEM((PIX, 6 * C), BF), pltpu.VMEM((PIX, C), F32), dma],
        4_000_000_000, 20_000_000,
        tp, targets.reshape(4, 128), labels, ro, u1, q1, c1, s1, u0, q0, c0, s0, s2, kernels,
    )
    got = lax.all_to_all(msg, "chan", 0, 0)
    hidden_grad = got[:, 192:224].reshape(8, 32, 8, OWN_COLS)
    hidden_grad = jnp.transpose(hidden_grad, (1, 2, 0, 3)).reshape(32, 8, 8 * OWN_COLS).astype(F32)
    part = call(
        corr_kernel,
        [VM, HB, HB],
        shape(16, 224, 128, dtype=BF),
        [
            pltpu.VMEM((8, V_ALL, C), BF), pltpu.VMEM((2, 8, 8, OWN_COLS, C), BF),
            pltpu.VMEM((288, 16 * OWN), BF), pltpu.SemaphoreType.DMA((2,)),
        ],
        4_000_000_000, 10_000_000,
        got, turned.reshape(2, 8, 8, OWN_COLS, C), vs,
    )
    mine = lax.all_to_all(part, "rows", 0, 0)
    last = (row_tile % 4 == 3).astype(jnp.int32)[None]
    mine = call(
        finish_sum_kernel, [SM, VM], shape(16, 224, 128, dtype=BF), [], 1_000_000, 2_000_000, last, mine,
        limit=16 * 1024 * 1024,
    )
    whole = lax.all_to_all(mine, "rows", 0, 0)
    gate_grad, readout_grad = call(
        layout_kernel, [VM], (shape(27, 32, 2 * C), shape(1, C)), [], 1_000_000, 3_000_000, whole,
        limit=16 * 1024 * 1024,
    )
    gate_grad = jnp.transpose(gate_grad.reshape(3, 9, 32, 2 * C), (0, 2, 1, 3))
    readout_grad = lax.dynamic_slice_in_dim(readout_grad[0], chan * 32, 32)
    return (loss[0, 0], gate_grad, readout_grad, hidden_grad)


def solution(mesh):
    in_specs = (
        P(None, None, "rows", None),
        P("chan", "rows", None),
        P(None, "chan", None, None),
        P("chan"),
        P("rows", None),
        P(),
    )
    out_specs = (P(), P(None, "chan", None, None), P("chan"), P("chan", "rows", None))
    return jax.shard_map(
        per_device, mesh=mesh, in_specs=in_specs, out_specs=out_specs, check_vma=False
    )
```

```python
import functools

import jax
import jax.numpy as jnp
from jax import lax
from jax.experimental import pallas as pl
from jax.experimental.pallas import tpu as pltpu
from jax.sharding import PartitionSpec as P

BF = jnp.bfloat16
F32 = jnp.float32
PITCH = 48
RIM = 8
ROWS_IN = 24
PIX = ROWS_IN * PITCH
OWN_COLS = 32
OWN = 8 * OWN_COLS
C = 256
K = 512
CUTS = 2
V_ROWS = 10 * OWN_COLS
V_ALL = 4 * V_ROWS + 4 * OWN_COLS
VMEM_LIMIT = 56 * 1024 * 1024


def sigmoid(x):
    return 0.5 * jnp.tanh(0.5 * x) + 0.5


class Taps:
    def __init__(self, ref, coming=None):
        self.ref, self.coming = ref, coming or {}

    def arrive(self, gate, a):
        if (gate, a) in self.coming:
            self.coming.pop((gate, a)).wait()

    def rows(self, gate, tap):
        block = self.ref[:, gate * 9 + tap]
        return block.reshape(C, block.shape[-1])


def put(dst, row, count, lane, stride, left_first, x):
    before = pltpu.roll(x, 1, axis=0)
    after = pltpu.roll(x, count - 1, axis=0)
    order = (before, x, after) if left_first else (after, x, before)
    for b in range(3):
        dst[row : row + count, b * stride + lane : b * stride + lane + C] = order[b].astype(BF)


def own_pixels(x):
    return x.reshape(8, PITCH, C)[:, RIM : RIM + OWN_COLS].reshape(OWN, C)


def wide(lab):
    return jnp.concatenate([lab, lab], axis=1)


def conv(xc, w, gates, start, count):
    total = None
    for a in range(3):
        lhs = xc[pl.ds(start + (a - 1) * PITCH, count), :]
        for g in gates:
            w.arrive(g, a)
        rhs = [jnp.concatenate([w.rows(g, 3 * a + b) for b in range(3)], axis=1) for g in gates]
        rhs = jnp.concatenate(rhs, axis=0) if len(rhs) > 1 else rhs[0]
        term = lax.dot_general(lhs, rhs, (((1,), (1,)), ((), ())), preferred_element_type=F32)
        total = term if total is None else total + term
    return total


def forward_kernel(
    above, middle, below, lab, ro, kernels,
    u1, q1, c1, s1, u0, q0, c0, wst, s0, s2, v, tot, w4, xc, ubs, qbs, cbs, sb, sems
):
    coming = {}
    for a in range(3):
        for g in range(2):
            coming[g, a] = (kernels.at[:, pl.ds(g * 9 + 3 * a, 3)], w4.at[:, pl.ds(g * 9 + 3 * a, 3)])
    coming[2, 0] = (kernels.at[:, 18:27], w4.at[:, 18:27])
    for n, (key, (src, dst)) in enumerate(coming.items()):
        coming[key] = pltpu.make_async_copy(src, dst, sems.at[8 + n])
        coming[key].start()
    w = Taps(w4, coming)
    leaving = []

    def leave(src, dst):
        leaving.append(pltpu.make_async_copy(src, dst, sems.at[len(leaving)]))
        leaving[-1].start()

    def window(k):
        parts = [ref[k * 8 * PITCH : (k + 1) * 8 * PITCH].astype(F32) for ref in (above, middle, below)]
        return jnp.concatenate(parts, axis=0)

    def halo_block(field):
        return field.reshape(10, PITCH, C)[:, RIM : RIM + OWN_COLS].reshape(10 * OWN_COLS, C).astype(BF)

    for step in range(2):
        for n, ref in enumerate((above, below)):
            line = (step * 8 + 7 - 7 * n) * PITCH
            at = 4 * V_ROWS + (2 * step + n) * OWN_COLS
            v[at : at + OWN_COLS] = ref[line : line + PITCH].astype(F32)[RIM : RIM + OWN_COLS].astype(BF)
    sb[...] = window(2)
    for step in range(2):
        ub, qb, cb = ubs.at[step], qbs.at[step], cbs.at[step]
        keep = pl.ds(6 * PITCH, 12 * PITCH) if step == 0 else pl.ds(4 * PITCH, 16 * PITCH)
        first = 1 + 2 * step
        count = (ROWS_IN - 2 * first) * PITCH
        start = first * PITCH
        put(xc, 0, PIX, 0, 2 * C, True, window(step))
        put(xc, 0, PIX, C, 2 * C, True, sb[...])
        piece = count // CUTS
        v[2 * step * V_ROWS : (2 * step + 1) * V_ROWS] = halo_block(sb[7 * PITCH : 17 * PITCH])
        for i in range(CUTS):
            at = start + i * piece
            both = sigmoid(conv(xc, w, (0, 1), at, piece))
            ub[at : at + piece] = both[:, :C]
            qb[at : at + piece] = both[:, C:]
        leave(ub.at[keep], (u0, u1)[step])
        leave(qb.at[keep], (q0, q1)[step])
        rs = (qb[start : start + count] * sb[start : start + count]).astype(BF).astype(F32)
        v[(2 * step + 1) * V_ROWS : (2 * step + 2) * V_ROWS] = halo_block(rs[(7 - first) * PITCH : (17 - first) * PITCH])
        put(xc, start, count, C, 2 * C, True, rs)
        start += PITCH
        count -= 2 * PITCH
        piece = count // CUTS
        for i in range(CUTS):
            at = start + i * piece
            cand = jnp.tanh(conv(xc, w, (2,), at, piece))
            u = ub[at : at + piece]
            s = sb[at : at + piece]
            nxt = (1.0 - u) * s + u * cand
            nxt = jnp.where(wide(lab[at : at + piece]) > 0, nxt, 0.0).astype(BF).astype(F32)
            cb[at : at + piece] = cand
            if step == 1:
                s1[at - 4 * PITCH : at - 4 * PITCH + piece] = s.astype(BF)
            sb[at : at + piece] = nxt
        leave(cb.at[keep], (c0, c1)[step])
        if step == 0:
            leave(w4.at[:, :, :, C:], wst)
    s0[...] = window(2)[6 * PITCH : 18 * PITCH].astype(BF)
    last = sb[8 * PITCH : 16 * PITCH]
    s2[...] = last.astype(BF)
    rain = jnp.sum(last * ro[...], axis=1, keepdims=True)
    labels = lab[8 * PITCH : 16 * PITCH]
    column = lax.rem(lax.broadcasted_iota(jnp.int32, labels.shape, 0), PITCH)
    labels = jnp.where((column >= RIM) & (column < RIM + OWN_COLS), labels, 0)
    lanes = lax.broadcasted_iota(jnp.int32, labels.shape, 1) + 1
    totals, counts = [], []
    for i in range(K // 128):
        hit = labels == lanes + 128 * i
        totals.append(jnp.sum(jnp.where(hit, rain, 0.0), axis=0, keepdims=True))
        counts.append(jnp.sum(jnp.where(hit, 1.0, 0.0), axis=0, keepdims=True))
    tot[...] = jnp.broadcast_to(jnp.concatenate(totals + counts, axis=0)[None], tot.shape)
    for sent in leaving:
        sent.wait()


def adjoint(px, w, gates, start, count):
    total = None
    width = len(gates) * C
    for a in range(3):
        lhs = px[pl.ds(start + (1 - a) * PITCH, count), : 3 * width]
        rhs = jnp.concatenate(
            [w.rows(g, 3 * a + b) for b in range(3) for g in gates], axis=0
        )
        term = jnp.dot(lhs, rhs, preferred_element_type=F32)
        total = term if total is None else total + term
    return total


def backward_kernel(
    tp, tgt, lab, ro, s1, s0, s2, hu1, hq1, hc1, hu0, hq0, hc0, kernels, msg, loss,
    w4, px, gs, u1, q1, c1, u0, q0, c0, sems
):
    pairs = [
        (hu1, u1), (hc1, c1), (kernels.at[:, 18:27], w4.at[:, 18:27]), (hq1, q1),
        (kernels.at[:, 0:18], w4.at[:, 0:18]), (hu0, u0), (hc0, c0), (hq0, q0),
    ]
    coming = [pltpu.make_async_copy(src, dst, sems.at[n]) for n, (src, dst) in enumerate(pairs)]
    for copy in coming:
        copy.start()

    def need(count):
        for _ in range(count):
            coming.pop(0).wait()

    w = Taps(w4)
    sums = jnp.sum(tp[...], axis=0)
    scale = 1.0 / (sums[4:8] + 1.0)
    mean = sums[0:4] * scale
    rate = jnp.maximum(mean, 0.0) + jnp.log1p(jnp.exp(-jnp.abs(mean)))
    miss = rate - tgt[...]
    loss[...] = jnp.broadcast_to(0.5 / K * jnp.sum(miss * miss), (8, 128))
    gm = miss * (1.0 / K) * (1.0 / (1.0 + jnp.exp(-mean))) * scale

    labels = lab[4 * PITCH : 20 * PITCH]
    lanes = lax.broadcasted_iota(jnp.int32, labels.shape, 1) + 1
    grain = jnp.zeros(labels.shape, F32)
    for i in range(K // 128):
        grain += jnp.where(labels == lanes + 128 * i, gm[i : i + 1], 0.0)
    grain = jnp.sum(grain, axis=1, keepdims=True)
    gs[4 * PITCH : 20 * PITCH] = grain * ro[...]
    part = s2[...].astype(F32) * grain[4 * PITCH : 12 * PITCH]
    column = lax.rem(lax.broadcasted_iota(jnp.int32, part.shape, 0), PITCH)
    part = jnp.where((column >= RIM) & (column < RIM + OWN_COLS), part, 0.0)
    part = jnp.sum(part, axis=0, keepdims=True)
    part_hi = part.astype(BF).astype(F32)
    tail = lax.broadcasted_iota(jnp.int32, (16, C), 0)
    tail = jnp.where(tail == 0, part_hi, jnp.where(tail == 1, part - part_hi, 0.0)).astype(BF)
    for j in range(8):
        msg[j, 224:240] = tail

    def send(slot, field):
        turned = own_pixels(field).T.astype(BF)
        for j in range(8):
            msg[j, slot * 32 : slot * 32 + 32] = turned[j * 32 : j * 32 + 32]

    for step in (1, 0):
        first = 4 if step == 1 else 6
        rows = ROWS_IN - 2 * first
        uv, qv, cv = (u1, q1, c1) if step == 1 else (u0, q0, c0)

        def state(lo, hi):
            if step == 1:
                return s1[(lo - 4) * PITCH : (hi - 4) * PITCH].astype(F32)
            return s0[(lo - 6) * PITCH : (hi - 6) * PITCH].astype(F32)

        def at(ref, lo, hi):
            return ref[(lo - first) * PITCH : (hi - first) * PITCH]

        lo, hi = first, first + rows
        need(2)
        g = gs[lo * PITCH : hi * PITCH]
        cand = cv[...]
        pc = (g * uv[...] * (1.0 - cand * cand)).astype(BF).astype(F32)
        put(px, lo * PITCH, rows * PITCH, 0, C, False, pc)
        send(step * 3 + 2, pc[(8 - lo) * PITCH : (16 - lo) * PITCH])
        lo, hi = lo + 1, hi - 1
        n = (hi - lo) * PITCH
        need(2 if step == 1 else 1)
        grs = adjoint(px, w, (2,), lo * PITCH, n)
        s = state(lo, hi)
        g = gs[lo * PITCH : hi * PITCH]
        u, q, cand = at(uv, lo, hi), at(qv, lo, hi), at(cv, lo, hi)
        pu = (g * (cand - s) * u * (1.0 - u)).astype(BF).astype(F32)
        pq = (grs * s * q * (1.0 - q)).astype(BF).astype(F32)
        gs[lo * PITCH : hi * PITCH] = g * (1.0 - u) + grs * q
        put(px, lo * PITCH, n, 0, 2 * C, False, pu)
        put(px, lo * PITCH, n, C, 2 * C, False, pq)
        send(step * 3, pu[(8 - lo) * PITCH : (16 - lo) * PITCH])
        send(step * 3 + 1, pq[(8 - lo) * PITCH : (16 - lo) * PITCH])
        lo, hi = lo + 1, hi - 1
        n = (hi - lo) * PITCH
        need(1 if step == 1 else 0)
        g = gs[lo * PITCH : hi * PITCH] + adjoint(px, w, (0, 1), lo * PITCH, n)
        g = jnp.where(wide(lab[lo * PITCH : hi * PITCH]) > 0, g, 0.0)
        if step == 1:
            gs[lo * PITCH : hi * PITCH] = g
        else:
            send(6, g)


def corr_kernel(r, vf, vs, out, p3):
    def lanes_of(j, t):
        return r[j, t * 96 : t * 96 + 96, :].astype(F32)

    column = lax.rem(lax.broadcasted_iota(jnp.int32, (96, OWN), 1), OWN_COLS)
    for t in range(2):
        for j in range(8):
            here = lanes_of(j, t)
            nxt = pltpu.roll(here, OWN - 1, axis=1)
            prv = pltpu.roll(here, 1, axis=1)
            over = pltpu.roll(lanes_of(j + 1, t), OWN_COLS - 1, axis=1) if j < 7 else jnp.zeros_like(here)
            under = pltpu.roll(lanes_of(j - 1, t), OWN - OWN_COLS + 1, axis=1) if j > 0 else jnp.zeros_like(here)
            nxt = jnp.where(column == OWN_COLS - 1, over, nxt)
            prv = jnp.where(column == 0, under, prv)
            at = (t * 8 + j) * OWN
            for b, field in enumerate((nxt, here, prv)):
                for g in range(3):
                    p3[g * 96 + b * 32 : g * 96 + b * 32 + 32, at : at + OWN] = field[
                        g * 32 : g * 32 + 32
                    ].astype(BF)

    def store(g, a, value, half):
        for b in range(3):
            slot = g * 9 + 3 * a + b
            for l in range(2):
                lane = half * 2 + l
                out[lane * 4 + slot // 7, (slot % 7) * 32 : (slot % 7) * 32 + 32] = value[
                    b * 32 : b * 32 + 32, l * 128 : l * 128 + 128
                ].astype(BF)

    def frame_rows(t, j, a):
        at = 4 * V_ROWS + 2 * t * OWN_COLS
        if a == 0:
            return vs[j, at : at + OWN_COLS], vf[t, 0:7, j].reshape(7 * OWN_COLS, C)
        if a == 1:
            return (vf[t, :, j].reshape(OWN, C),)
        return vf[t, 1:8, j].reshape(7 * OWN_COLS, C), vs[j, at + OWN_COLS : at + 2 * OWN_COLS]

    order = [(t, j) for t in range(2) for j in range(8)]
    for a in range(3):
        field = jnp.concatenate([part for t, j in order for part in frame_rows(t, j, a)], axis=0)
        value = jnp.dot(p3[...], field, preferred_element_type=F32)
        for g in range(3):
            store(g, a, value[g * 96 : g * 96 + 96], 0)
        field = jnp.concatenate([vs[j, pl.ds(2 * t * V_ROWS + a * OWN_COLS, OWN)] for t, j in order], axis=0)
        value = jnp.dot(p3[0:192], field, preferred_element_type=F32)
        for g in range(2):
            store(g, a, value[g * 96 : g * 96 + 96], 1)
        field = jnp.concatenate([vs[j, pl.ds((2 * t + 1) * V_ROWS + a * OWN_COLS, OWN)] for t, j in order], axis=0)
        value = jnp.dot(p3[192:288], field, preferred_element_type=F32)
        store(2, a, value, 1)

    tail = jnp.sum(r[:, 224:240, :].astype(F32), axis=0)
    part = tail[0:1] + tail[1:2]
    part_hi = part.astype(BF).astype(F32)
    row = lax.broadcasted_iota(jnp.int32, (32, C), 0)
    last = jnp.where(row == 0, part_hi, jnp.where(row == 1, part - part_hi, 0.0)).astype(BF)
    for l in range(2):
        out[l * 4 + 3, 192:224] = last[:, l * 128 : l * 128 + 128]
        out[l * 4 + 11, 192:224] = jnp.zeros((32, 128), BF)


def finish_sum_kernel(last, parts, out):
    total = parts[0].astype(F32)
    for n in range(1, 16):
        total = total + parts[n].astype(F32)
    pair = total[192:193] + total[193:194]
    pair_hi = pair.astype(BF).astype(F32)
    row = lax.broadcasted_iota(jnp.int32, total.shape, 0)
    split = jnp.where(row == 192, pair_hi, jnp.where(row == 193, pair - pair_hi, total))
    total = jnp.where(last[0] == 1, split, total).astype(BF)
    out[...] = jnp.broadcast_to(total[None], out.shape)


def layout_kernel(parts, grad, readout):
    for lane in range(4):
        for group in range(4):
            block = parts[lane * 4 + group].astype(F32).reshape(7, 32, 128)
            count = min(7, 27 - group * 7)
            grad[group * 7 : group * 7 + count, :, lane * 128 : lane * 128 + 128] = block[:count]
            if group == 3 and lane < 2:
                readout[:, lane * 128 : lane * 128 + 128] = block[6, 0:1] + block[6, 1:2]


VM = pl.BlockSpec(memory_space=pltpu.VMEM)
SM = pl.BlockSpec(memory_space=pltpu.SMEM)
HB = pl.BlockSpec(memory_space=pl.ANY)


def call(kernel, specs, outs, scratch, flops, moved, *args, limit=VMEM_LIMIT, out_specs=None):
    return pl.pallas_call(
        kernel,
        out_shape=outs,
        in_specs=specs,
        out_specs=jax.tree.map(lambda _: VM, outs) if out_specs is None else out_specs,
        scratch_shapes=scratch,
        compiler_params=pltpu.CompilerParams(vmem_limit_bytes=limit),
        cost_estimate=pl.CostEstimate(flops=flops, bytes_accessed=moved, transcendentals=0),
    )(*args)


def shape(*dims, dtype=F32):
    return jax.ShapeDtypeStruct(dims, dtype)


def columns_window(field, axis, at):
    widths = [(0, 0)] * field.ndim
    widths[axis] = (RIM, RIM)
    return lax.dynamic_slice_in_dim(jnp.pad(field, widths), at, PITCH, axis=axis)


def per_device(frames, hidden_init, gate_weight, readout, catchment, targets):
    chan = lax.axis_index("chan")
    row_tile = lax.axis_index("rows")
    up = [(i, i + 1) for i in range(15)]
    down = [(i + 1, i) for i in range(15)]

    padded = jnp.pad(hidden_init, ((0, 0), (0, 0), (RIM, RIM)))
    pieces = jnp.stack([padded[:, :, 32 * j : 32 * j + PITCH] for j in range(8)])
    own_readout = jnp.broadcast_to(jnp.pad(readout, (0, 8 * PITCH - 32)), (8, 1, 8 * PITCH))
    pieces = jnp.concatenate([pieces.reshape(8, 32, 8 * PITCH), own_readout], axis=1)
    own_kernel = jnp.transpose(gate_weight, (0, 2, 1, 3)).reshape(27, 32, 2 * C)
    kernels = lax.all_gather(own_kernel, "chan", axis=0)
    pieces = lax.all_to_all(pieces, "chan", 0, 0)
    turned = jnp.transpose(frames, (0, 2, 3, 1))
    ro = pieces[:, 32, :32].reshape(1, C).astype(F32)
    state = jnp.transpose(pieces[:, :32].reshape(C, 8 * PITCH))
    labels = columns_window(catchment + 1, 1, 32 * chan).reshape(-1)
    digits = jnp.concatenate([labels // 256, labels % 256]).astype(BF).reshape(3, C)
    middle = columns_window(turned, 2, 32 * chan).reshape(16 * PITCH, C)
    middle = jnp.concatenate([middle, state, jnp.pad(digits, ((0, 13), (0, 0)))], axis=0)
    above = lax.ppermute(middle, "rows", up)
    below = lax.ppermute(middle, "rows", down)
    digits = jnp.stack([part[24 * PITCH : 24 * PITCH + 3] for part in (above, middle, below)])
    digits = digits.reshape(3, 2, 8 * PITCH).astype(jnp.int32)
    labels = (digits[:, 0] * 256 + digits[:, 1]).reshape(PIX, 1)
    labels = jnp.broadcast_to(labels, (PIX, 128))

    n1, n0 = 16 * PITCH, 12 * PITCH
    u1, q1, c1, s1, u0, q0, c0, wst, s0, s2, v, tot = call(
        forward_kernel,
        [VM] * 5 + [HB],
        (
            shape(n1, C), shape(n1, C), shape(n1, C), shape(n1, C, dtype=BF),
            shape(n0, C), shape(n0, C), shape(n0, C), shape(8, 27, 32, C, dtype=BF), shape(n0, C, dtype=BF), shape(8 * PITCH, C, dtype=BF),
            shape(V_ALL, C, dtype=BF), shape(128, 8, 128),
        ),
        [pltpu.VMEM((8, 27, 32, 2 * C), BF), pltpu.VMEM((PIX, 6 * C), BF)]
        + [pltpu.VMEM((2, PIX, C), F32)] * 3 + [pltpu.VMEM((PIX, C), F32), pltpu.SemaphoreType.DMA((15,))],
        13_000_000_000, 20_000_000,
        above, middle, below, labels, ro, kernels,
        out_specs=(HB, HB, HB, VM, HB, HB, HB, HB) + (VM,) * 4,
    )
    tp = lax.all_to_all(tot, ("rows", "chan"), 0, 0)
    vs = lax.all_gather(v, "chan", axis=0)
    msg, loss = call(
        backward_kernel,
        [VM] * 7 + [HB] * 7,
        (shape(8, 240, C, dtype=BF), shape(8, 128)),
        [pltpu.VMEM((8, 27, 32, C), BF), pltpu.VMEM((PIX, 6 * C), BF), pltpu.VMEM((PIX, C), F32)]
        + [pltpu.VMEM((n, C), F32) for n in (n1, n1, n1, n0, n0, n0)] + [pltpu.SemaphoreType.DMA((8,))],
        4_000_000_000, 20_000_000,
        tp, targets.reshape(4, 128), labels, ro, s1, s0, s2,
        u1, q1, c1, u0, q0, c0, wst,
    )
    got = lax.all_to_all(msg, "chan", 0, 0)
    hidden_grad = got[:, 192:224].reshape(8, 32, 8, OWN_COLS)
    hidden_grad = jnp.transpose(hidden_grad, (1, 2, 0, 3)).reshape(32, 8, 8 * OWN_COLS).astype(F32)
    part = call(
        corr_kernel,
        [VM] * 3,
        shape(16, 224, 128, dtype=BF),
        [pltpu.VMEM((288, 16 * OWN), BF)],
        4_000_000_000, 10_000_000,
        got, turned.reshape(2, 8, 8, OWN_COLS, C), vs,
        limit=24 * 1024 * 1024,
    )
    mine = lax.all_to_all(part, "rows", 0, 0)
    last = (row_tile % 4 == 3).astype(jnp.int32)[None]
    mine = call(
        finish_sum_kernel, [SM, VM], shape(16, 224, 128, dtype=BF), [], 1_000_000, 2_000_000, last, mine,
        limit=16 * 1024 * 1024,
    )
    whole = lax.all_to_all(mine, "rows", 0, 0)
    gate_grad, readout_grad = call(
        layout_kernel, [VM], (shape(27, 32, 2 * C), shape(1, C)), [], 1_000_000, 3_000_000, whole,
        limit=16 * 1024 * 1024,
    )
    gate_grad = jnp.transpose(gate_grad.reshape(3, 9, 32, 2 * C), (0, 2, 1, 3))
    readout_grad = lax.dynamic_slice_in_dim(readout_grad[0], chan * 32, 32)
    return (loss[0, 0], gate_grad, readout_grad, hidden_grad)


def solution(mesh):
    in_specs = (
        P(None, None, "rows", None),
        P("chan", "rows", None),
        P(None, "chan", None, None),
        P("chan"),
        P("rows", None),
        P(),
    )
    out_specs = (P(), P(None, "chan", None, None), P("chan"), P("chan", "rows", None))
    return jax.shard_map(
        per_device, mesh=mesh, in_specs=in_specs, out_specs=out_specs, check_vma=False
    )
```

```python
import functools

import jax
import jax.numpy as jnp
from jax import lax
from jax.experimental import pallas as pl
from jax.experimental.pallas import tpu as pltpu
from jax.sharding import PartitionSpec as P

BF = jnp.bfloat16
F32 = jnp.float32
PITCH = 48
RIM = 8
ROWS_IN = 24
PIX = ROWS_IN * PITCH
OWN_COLS = 32
OWN = 8 * OWN_COLS
C = 256
K = 512
CUTS = 2
V_ROWS = 10 * OWN_COLS
V_ALL = 4 * V_ROWS + 4 * OWN_COLS
VMEM_LIMIT = 56 * 1024 * 1024


def sigmoid(x):
    return 0.5 * jnp.tanh(0.5 * x) + 0.5


class Taps:
    def __init__(self, ref, coming=None):
        self.ref, self.coming = ref, coming or {}

    def arrive(self, gate, a):
        if (gate, a) in self.coming:
            self.coming.pop((gate, a)).wait()

    def rows(self, gate, tap):
        block = self.ref[:, gate * 9 + tap]
        return block.reshape(C, block.shape[-1])


def put(dst, row, count, lane, stride, left_first, x):
    before = pltpu.roll(x, 1, axis=0)
    after = pltpu.roll(x, count - 1, axis=0)
    order = (before, x, after) if left_first else (after, x, before)
    for b in range(3):
        dst[row : row + count, b * stride + lane : b * stride + lane + C] = order[b].astype(BF)


def own_pixels(x):
    return x.reshape(8, PITCH, C)[:, RIM : RIM + OWN_COLS].reshape(OWN, C)


def wide(lab):
    return jnp.concatenate([lab, lab], axis=1)


def conv(xc, w, gates, start, count):
    total = None
    for a in range(3):
        lhs = xc[pl.ds(start + (a - 1) * PITCH, count), :]
        for g in gates:
            w.arrive(g, a)
        rhs = [jnp.concatenate([w.rows(g, 3 * a + b) for b in range(3)], axis=1) for g in gates]
        rhs = jnp.concatenate(rhs, axis=0) if len(rhs) > 1 else rhs[0]
        term = lax.dot_general(lhs, rhs, (((1,), (1,)), ((), ())), preferred_element_type=F32)
        total = term if total is None else total + term
    return total


def forward_kernel(
    above, middle, below, lab, ro, kernels,
    u1, q1, c1, s1, u0, q0, c0, wst, s0, s2, v, tot, w4, xc, ubs, qbs, cbs, sb, sems
):
    coming = {}
    for a in range(3):
        for g in range(2):
            coming[g, a] = (kernels.at[:, pl.ds(g * 9 + 3 * a, 3)], w4.at[:, pl.ds(g * 9 + 3 * a, 3)])
    coming[2, 0] = (kernels.at[:, 18:27], w4.at[:, 18:27])
    for n, (key, (src, dst)) in enumerate(coming.items()):
        coming[key] = pltpu.make_async_copy(src, dst, sems.at[8 + n])
        coming[key].start()
    w = Taps(w4, coming)
    leaving = []

    def leave(src, dst):
        leaving.append(pltpu.make_async_copy(src, dst, sems.at[len(leaving)]))
        leaving[-1].start()

    def window(k):
        parts = [ref[k * 8 * PITCH : (k + 1) * 8 * PITCH].astype(F32) for ref in (above, middle, below)]
        return jnp.concatenate(parts, axis=0)

    def halo_block(field):
        return field.reshape(10, PITCH, C)[:, RIM : RIM + OWN_COLS].reshape(10 * OWN_COLS, C).astype(BF)

    for step in range(2):
        for n, ref in enumerate((above, below)):
            line = (step * 8 + 7 - 7 * n) * PITCH
            at = 4 * V_ROWS + (2 * step + n) * OWN_COLS
            v[at : at + OWN_COLS] = ref[line : line + PITCH].astype(F32)[RIM : RIM + OWN_COLS].astype(BF)
    sb[...] = window(2)
    for step in range(2):
        ub, qb, cb = ubs.at[step], qbs.at[step], cbs.at[step]
        keep = pl.ds(6 * PITCH, 12 * PITCH) if step == 0 else pl.ds(4 * PITCH, 16 * PITCH)
        first = 1 + 2 * step
        count = (ROWS_IN - 2 * first) * PITCH
        start = first * PITCH
        put(xc, 0, PIX, 0, 2 * C, True, window(step))
        put(xc, 0, PIX, C, 2 * C, True, sb[...])
        piece = count // CUTS
        v[2 * step * V_ROWS : (2 * step + 1) * V_ROWS] = halo_block(sb[7 * PITCH : 17 * PITCH])
        for i in range(CUTS):
            at = start + i * piece
            both = sigmoid(conv(xc, w, (0, 1), at, piece))
            ub[at : at + piece] = both[:, :C]
            qb[at : at + piece] = both[:, C:]
        leave(ub.at[keep], (u0, u1)[step])
        leave(qb.at[keep], (q0, q1)[step])
        rs = (qb[start : start + count] * sb[start : start + count]).astype(BF).astype(F32)
        v[(2 * step + 1) * V_ROWS : (2 * step + 2) * V_ROWS] = halo_block(rs[(7 - first) * PITCH : (17 - first) * PITCH])
        put(xc, start, count, C, 2 * C, True, rs)
        start += PITCH
        count -= 2 * PITCH
        piece = count // CUTS
        for i in range(CUTS):
            at = start + i * piece
            cand = jnp.tanh(conv(xc, w, (2,), at, piece))
            u = ub[at : at + piece]
            s = sb[at : at + piece]
            nxt = (1.0 - u) * s + u * cand
            nxt = jnp.where(wide(lab[at : at + piece]) > 0, nxt, 0.0).astype(BF).astype(F32)
            cb[at : at + piece] = cand
            if step == 1:
                s1[at - 4 * PITCH : at - 4 * PITCH + piece] = s.astype(BF)
            sb[at : at + piece] = nxt
        leave(cb.at[keep], (c0, c1)[step])
        if step == 0:
            leave(w4.at[:, :, :, C:], wst)
    s0[...] = window(2)[6 * PITCH : 18 * PITCH].astype(BF)
    last = sb[8 * PITCH : 16 * PITCH]
    s2[...] = last.astype(BF)
    rain = jnp.sum(last * ro[...], axis=1, keepdims=True)
    labels = lab[8 * PITCH : 16 * PITCH]
    column = lax.rem(lax.broadcasted_iota(jnp.int32, labels.shape, 0), PITCH)
    labels = jnp.where((column >= RIM) & (column < RIM + OWN_COLS), labels, 0)
    lanes = lax.broadcasted_iota(jnp.int32, labels.shape, 1) + 1
    totals, counts = [], []
    for i in range(K // 128):
        hit = labels == lanes + 128 * i
        totals.append(jnp.sum(jnp.where(hit, rain, 0.0), axis=0, keepdims=True))
        counts.append(jnp.sum(jnp.where(hit, 1.0, 0.0), axis=0, keepdims=True))
    tot[...] = jnp.broadcast_to(jnp.concatenate(totals + counts, axis=0)[None], tot.shape)
    for sent in leaving:
        sent.wait()


def adjoint(px, w, gates, start, count):
    half = count // 2
    return jnp.concatenate([adjoint_rows(px, w, gates, at, half) for at in (start, start + half)], axis=0)


def adjoint_rows(px, w, gates, start, count):
    total = None
    width = len(gates) * C
    for a in range(3):
        lhs = px[pl.ds(start + (1 - a) * PITCH, count), : 3 * width]
        rhs = jnp.concatenate(
            [w.rows(g, 3 * a + b) for b in range(3) for g in gates], axis=0
        )
        term = jnp.dot(lhs, rhs, preferred_element_type=F32)
        total = term if total is None else total + term
    return total


def backward_kernel(
    tp, tgt, lab, ro, s1, s0, s2, hu1, hq1, hc1, hu0, hq0, hc0, kernels, msg, loss,
    w4, px, gs, u1, q1, c1, u0, q0, c0, sems
):
    pairs = [
        (hu1, u1), (hc1, c1), (kernels.at[:, 18:27], w4.at[:, 18:27]), (hq1, q1),
        (kernels.at[:, 0:18], w4.at[:, 0:18]), (hu0, u0), (hc0, c0), (hq0, q0),
    ]
    coming = [pltpu.make_async_copy(src, dst, sems.at[n]) for n, (src, dst) in enumerate(pairs)]
    for copy in coming:
        copy.start()

    def need(count):
        for _ in range(count):
            coming.pop(0).wait()

    w = Taps(w4)
    sums = jnp.sum(tp[...], axis=0)
    scale = 1.0 / (sums[4:8] + 1.0)
    mean = sums[0:4] * scale
    rate = jnp.maximum(mean, 0.0) + jnp.log1p(jnp.exp(-jnp.abs(mean)))
    miss = rate - tgt[...]
    loss[...] = jnp.broadcast_to(0.5 / K * jnp.sum(miss * miss), (8, 128))
    gm = miss * (1.0 / K) * (1.0 / (1.0 + jnp.exp(-mean))) * scale

    labels = lab[4 * PITCH : 20 * PITCH]
    lanes = lax.broadcasted_iota(jnp.int32, labels.shape, 1) + 1
    grain = jnp.zeros(labels.shape, F32)
    for i in range(K // 128):
        grain += jnp.where(labels == lanes + 128 * i, gm[i : i + 1], 0.0)
    grain = jnp.sum(grain, axis=1, keepdims=True)
    gs[4 * PITCH : 20 * PITCH] = grain * ro[...]
    part = s2[...].astype(F32) * grain[4 * PITCH : 12 * PITCH]
    column = lax.rem(lax.broadcasted_iota(jnp.int32, part.shape, 0), PITCH)
    part = jnp.where((column >= RIM) & (column < RIM + OWN_COLS), part, 0.0)
    part = jnp.sum(part, axis=0, keepdims=True)
    part_hi = part.astype(BF).astype(F32)
    tail = lax.broadcasted_iota(jnp.int32, (16, C), 0)
    tail = jnp.where(tail == 0, part_hi, jnp.where(tail == 1, part - part_hi, 0.0)).astype(BF)
    for j in range(8):
        msg[j, 224:240] = tail

    def send(slot, field):
        turned = own_pixels(field).T.astype(BF)
        for j in range(8):
            msg[j, slot * 32 : slot * 32 + 32] = turned[j * 32 : j * 32 + 32]

    for step in (1, 0):
        first = 4 if step == 1 else 6
        rows = ROWS_IN - 2 * first
        uv, qv, cv = (u1, q1, c1) if step == 1 else (u0, q0, c0)

        def state(lo, hi):
            if step == 1:
                return s1[(lo - 4) * PITCH : (hi - 4) * PITCH].astype(F32)
            return s0[(lo - 6) * PITCH : (hi - 6) * PITCH].astype(F32)

        def at(ref, lo, hi):
            return ref[(lo - first) * PITCH : (hi - first) * PITCH]

        lo, hi = first, first + rows
        need(2)
        g = gs[lo * PITCH : hi * PITCH]
        cand = cv[...]
        pc = (g * uv[...] * (1.0 - cand * cand)).astype(BF).astype(F32)
        put(px, lo * PITCH, rows * PITCH, 0, C, False, pc)
        send(step * 3 + 2, pc[(8 - lo) * PITCH : (16 - lo) * PITCH])
        lo, hi = lo + 1, hi - 1
        n = (hi - lo) * PITCH
        need(2 if step == 1 else 1)
        grs = adjoint(px, w, (2,), lo * PITCH, n)
        s = state(lo, hi)
        g = gs[lo * PITCH : hi * PITCH]
        u, q, cand = at(uv, lo, hi), at(qv, lo, hi), at(cv, lo, hi)
        pu = (g * (cand - s) * u * (1.0 - u)).astype(BF).astype(F32)
        pq = (grs * s * q * (1.0 - q)).astype(BF).astype(F32)
        gs[lo * PITCH : hi * PITCH] = g * (1.0 - u) + grs * q
        put(px, lo * PITCH, n, 0, 2 * C, False, pu)
        put(px, lo * PITCH, n, C, 2 * C, False, pq)
        send(step * 3, pu[(8 - lo) * PITCH : (16 - lo) * PITCH])
        send(step * 3 + 1, pq[(8 - lo) * PITCH : (16 - lo) * PITCH])
        lo, hi = lo + 1, hi - 1
        n = (hi - lo) * PITCH
        need(1 if step == 1 else 0)
        g = gs[lo * PITCH : hi * PITCH] + adjoint(px, w, (0, 1), lo * PITCH, n)
        g = jnp.where(wide(lab[lo * PITCH : hi * PITCH]) > 0, g, 0.0)
        if step == 1:
            gs[lo * PITCH : hi * PITCH] = g
        else:
            send(6, g)


def corr_kernel(r, vf, vs, out, p3):
    def lanes_of(j, t):
        return r[j, t * 96 : t * 96 + 96, :].astype(F32)

    column = lax.rem(lax.broadcasted_iota(jnp.int32, (96, OWN), 1), OWN_COLS)
    for t in range(2):
        for j in range(8):
            here = lanes_of(j, t)
            nxt = pltpu.roll(here, OWN - 1, axis=1)
            prv = pltpu.roll(here, 1, axis=1)
            over = pltpu.roll(lanes_of(j + 1, t), OWN_COLS - 1, axis=1) if j < 7 else jnp.zeros_like(here)
            under = pltpu.roll(lanes_of(j - 1, t), OWN - OWN_COLS + 1, axis=1) if j > 0 else jnp.zeros_like(here)
            nxt = jnp.where(column == OWN_COLS - 1, over, nxt)
            prv = jnp.where(column == 0, under, prv)
            at = (t * 8 + j) * OWN
            for b, field in enumerate((nxt, here, prv)):
                for g in range(3):
                    p3[g * 96 + b * 32 : g * 96 + b * 32 + 32, at : at + OWN] = field[
                        g * 32 : g * 32 + 32
                    ].astype(BF)

    def store(g, a, value, half):
        for b in range(3):
            slot = g * 9 + 3 * a + b
            for l in range(2):
                lane = half * 2 + l
                out[lane * 4 + slot // 7, (slot % 7) * 32 : (slot % 7) * 32 + 32] = value[
                    b * 32 : b * 32 + 32, l * 128 : l * 128 + 128
                ].astype(BF)

    def frame_rows(t, j, a):
        at = 4 * V_ROWS + 2 * t * OWN_COLS
        if a == 0:
            return vs[j, at : at + OWN_COLS], vf[t, 0:7, j].reshape(7 * OWN_COLS, C)
        if a == 1:
            return (vf[t, :, j].reshape(OWN, C),)
        return vf[t, 1:8, j].reshape(7 * OWN_COLS, C), vs[j, at + OWN_COLS : at + 2 * OWN_COLS]

    order = [(t, j) for t in range(2) for j in range(8)]
    for a in range(3):
        field = jnp.concatenate([part for t, j in order for part in frame_rows(t, j, a)], axis=0)
        value = jnp.dot(p3[...], field, preferred_element_type=F32)
        for g in range(3):
            store(g, a, value[g * 96 : g * 96 + 96], 0)
        field = jnp.concatenate([vs[j, pl.ds(2 * t * V_ROWS + a * OWN_COLS, OWN)] for t, j in order], axis=0)
        value = jnp.dot(p3[0:192], field, preferred_element_type=F32)
        for g in range(2):
            store(g, a, value[g * 96 : g * 96 + 96], 1)
        field = jnp.concatenate([vs[j, pl.ds((2 * t + 1) * V_ROWS + a * OWN_COLS, OWN)] for t, j in order], axis=0)
        value = jnp.dot(p3[192:288], field, preferred_element_type=F32)
        store(2, a, value, 1)

    tail = jnp.sum(r[:, 224:240, :].astype(F32), axis=0)
    part = tail[0:1] + tail[1:2]
    part_hi = part.astype(BF).astype(F32)
    row = lax.broadcasted_iota(jnp.int32, (32, C), 0)
    last = jnp.where(row == 0, part_hi, jnp.where(row == 1, part - part_hi, 0.0)).astype(BF)
    for l in range(2):
        out[l * 4 + 3, 192:224] = last[:, l * 128 : l * 128 + 128]
        out[l * 4 + 11, 192:224] = jnp.zeros((32, 128), BF)


def finish_sum_kernel(last, parts, out):
    total = parts[0].astype(F32)
    for n in range(1, 16):
        total = total + parts[n].astype(F32)
    pair = total[192:193] + total[193:194]
    pair_hi = pair.astype(BF).astype(F32)
    row = lax.broadcasted_iota(jnp.int32, total.shape, 0)
    split = jnp.where(row == 192, pair_hi, jnp.where(row == 193, pair - pair_hi, total))
    total = jnp.where(last[0] == 1, split, total).astype(BF)
    out[...] = jnp.broadcast_to(total[None], out.shape)


def layout_kernel(parts, grad, readout):
    for lane in range(4):
        for group in range(4):
            block = parts[lane * 4 + group].astype(F32).reshape(7, 32, 128)
            count = min(7, 27 - group * 7)
            grad[group * 7 : group * 7 + count, :, lane * 128 : lane * 128 + 128] = block[:count]
            if group == 3 and lane < 2:
                readout[:, lane * 128 : lane * 128 + 128] = block[6, 0:1] + block[6, 1:2]


VM = pl.BlockSpec(memory_space=pltpu.VMEM)
SM = pl.BlockSpec(memory_space=pltpu.SMEM)
HB = pl.BlockSpec(memory_space=pl.ANY)


def call(kernel, specs, outs, scratch, flops, moved, *args, limit=VMEM_LIMIT, out_specs=None):
    return pl.pallas_call(
        kernel,
        out_shape=outs,
        in_specs=specs,
        out_specs=jax.tree.map(lambda _: VM, outs) if out_specs is None else out_specs,
        scratch_shapes=scratch,
        compiler_params=pltpu.CompilerParams(vmem_limit_bytes=limit),
        cost_estimate=pl.CostEstimate(flops=flops, bytes_accessed=moved, transcendentals=0),
    )(*args)


def shape(*dims, dtype=F32):
    return jax.ShapeDtypeStruct(dims, dtype)


def columns_window(field, axis, at):
    widths = [(0, 0)] * field.ndim
    widths[axis] = (RIM, RIM)
    return lax.dynamic_slice_in_dim(jnp.pad(field, widths), at, PITCH, axis=axis)


def per_device(frames, hidden_init, gate_weight, readout, catchment, targets):
    chan = lax.axis_index("chan")
    row_tile = lax.axis_index("rows")
    up = [(i, i + 1) for i in range(15)]
    down = [(i + 1, i) for i in range(15)]

    padded = jnp.pad(hidden_init, ((0, 0), (0, 0), (RIM, RIM)))
    pieces = jnp.stack([padded[:, :, 32 * j : 32 * j + PITCH] for j in range(8)])
    own_readout = jnp.broadcast_to(jnp.pad(readout, (0, 8 * PITCH - 32)), (8, 1, 8 * PITCH))
    pieces = jnp.concatenate([pieces.reshape(8, 32, 8 * PITCH), own_readout], axis=1)
    own_kernel = jnp.transpose(gate_weight, (0, 2, 1, 3)).reshape(27, 32, 2 * C)
    kernels = lax.all_gather(own_kernel, "chan", axis=0)
    pieces = lax.all_to_all(pieces, "chan", 0, 0)
    turned = jnp.transpose(frames, (0, 2, 3, 1))
    ro = pieces[:, 32, :32].reshape(1, C).astype(F32)
    state = jnp.transpose(pieces[:, :32].reshape(C, 8 * PITCH))
    labels = columns_window(catchment + 1, 1, 32 * chan).reshape(-1)
    digits = jnp.concatenate([labels // 256, labels % 256]).astype(BF).reshape(3, C)
    middle = columns_window(turned, 2, 32 * chan).reshape(16 * PITCH, C)
    middle = jnp.concatenate([middle, state, jnp.pad(digits, ((0, 13), (0, 0)))], axis=0)
    above = lax.ppermute(middle, "rows", up)
    below = lax.ppermute(middle, "rows", down)
    digits = jnp.stack([part[24 * PITCH : 24 * PITCH + 3] for part in (above, middle, below)])
    digits = digits.reshape(3, 2, 8 * PITCH).astype(jnp.int32)
    labels = (digits[:, 0] * 256 + digits[:, 1]).reshape(PIX, 1)
    labels = jnp.broadcast_to(labels, (PIX, 128))

    n1, n0 = 16 * PITCH, 12 * PITCH
    u1, q1, c1, s1, u0, q0, c0, wst, s0, s2, v, tot = call(
        forward_kernel,
        [VM] * 5 + [HB],
        (
            shape(n1, C), shape(n1, C), shape(n1, C), shape(n1, C, dtype=BF),
            shape(n0, C), shape(n0, C), shape(n0, C), shape(8, 27, 32, C, dtype=BF), shape(n0, C, dtype=BF), shape(8 * PITCH, C, dtype=BF),
            shape(V_ALL, C, dtype=BF), shape(128, 8, 128),
        ),
        [pltpu.VMEM((8, 27, 32, 2 * C), BF), pltpu.VMEM((PIX, 6 * C), BF)]
        + [pltpu.VMEM((2, PIX, C), F32)] * 3 + [pltpu.VMEM((PIX, C), F32), pltpu.SemaphoreType.DMA((15,))],
        13_000_000_000, 20_000_000,
        above, middle, below, labels, ro, kernels,
        out_specs=(HB, HB, HB, VM, HB, HB, HB, HB) + (VM,) * 4,
    )
    tp = lax.all_to_all(tot, ("rows", "chan"), 0, 0)
    vs = lax.all_gather(v, "chan", axis=0)
    msg, loss = call(
        backward_kernel,
        [VM] * 7 + [HB] * 7,
        (shape(8, 240, C, dtype=BF), shape(8, 128)),
        [pltpu.VMEM((8, 27, 32, C), BF), pltpu.VMEM((PIX, 6 * C), BF), pltpu.VMEM((PIX, C), F32)]
        + [pltpu.VMEM((n, C), F32) for n in (n1, n1, n1, n0, n0, n0)] + [pltpu.SemaphoreType.DMA((8,))],
        4_000_000_000, 20_000_000,
        tp, targets.reshape(4, 128), labels, ro, s1, s0, s2,
        u1, q1, c1, u0, q0, c0, wst,
    )
    got = lax.all_to_all(msg, "chan", 0, 0)
    hidden_grad = got[:, 192:224].reshape(8, 32, 8, OWN_COLS)
    hidden_grad = jnp.transpose(hidden_grad, (1, 2, 0, 3)).reshape(32, 8, 8 * OWN_COLS).astype(F32)
    part = call(
        corr_kernel,
        [VM] * 3,
        shape(16, 224, 128, dtype=BF),
        [pltpu.VMEM((288, 16 * OWN), BF)],
        4_000_000_000, 10_000_000,
        got, turned.reshape(2, 8, 8, OWN_COLS, C), vs,
        limit=24 * 1024 * 1024,
    )
    mine = lax.all_to_all(part, "rows", 0, 0)
    last = (row_tile % 4 == 3).astype(jnp.int32)[None]
    mine = call(
        finish_sum_kernel, [SM, VM], shape(16, 224, 128, dtype=BF), [], 1_000_000, 2_000_000, last, mine,
        limit=16 * 1024 * 1024,
    )
    whole = lax.all_to_all(mine, "rows", 0, 0)
    gate_grad, readout_grad = call(
        layout_kernel, [VM], (shape(27, 32, 2 * C), shape(1, C)), [], 1_000_000, 3_000_000, whole,
        limit=16 * 1024 * 1024,
    )
    gate_grad = jnp.transpose(gate_grad.reshape(3, 9, 32, 2 * C), (0, 2, 1, 3))
    readout_grad = lax.dynamic_slice_in_dim(readout_grad[0], chan * 32, 32)
    return (loss[0, 0], gate_grad, readout_grad, hidden_grad)


def solution(mesh):
    in_specs = (
        P(None, None, "rows", None),
        P("chan", "rows", None),
        P(None, "chan", None, None),
        P("chan"),
        P("rows", None),
        P(),
    )
    out_specs = (P(), P(None, "chan", None, None), P("chan"), P("chan", "rows", None))
    return jax.shard_map(
        per_device, mesh=mesh, in_specs=in_specs, out_specs=out_specs, check_vma=False
    )
```
